256 devices in a mesh: chaos: 2 (over x_hi), azim: 32 (over z, y), axial: 4 (over x_lo, core).
Axes of the slice: x: 4 (x_hi: 2, x_lo: 2; x = x_hi * 2 + x_lo), y: 4, z: 8, core: 2. Of those that a mesh axis runs over, the one named last changes fastest.
Arguments:
- displacement: float32 [36, 3, 128, 128, 128], P('chaos', None, 'axial', 'azim'), may hold values from -6 to 6
- mean_modulus: float32 [128, 128, 128], P('axial', 'azim'), may hold values from 0.5 to 2
- kl_fields: float32 [7, 128, 128, 128], P(None, 'axial', 'azim'), may hold values from -4 to 4
- triple_cols: int32 [8, 36, 4], replicated, may hold values from 0 to 35, as said below
- triple_vals: float32 [8, 36, 4], replicated, may hold values from -1.5 to 1.5
Outputs:
- response: float32 [36, 3, 128, 128, 128], P('chaos', None, 'axial', 'azim')
The draws below stay inside these ranges and needn't reach their ends.
Inputs may be any that keep to these rules, and one draw needn't show every extreme that they name: `triple_cols`: the 4 entries of one row are distinct; for expansion term 0 the first entry of row i is i.
All inputs are finite; a program needn't handle non-finite values.
Results may differ from the reference program's by a relative error of at most 0.0001.
Values sent between devices are 32-bit elements; how exact they have to be, the bound alone decides.
A program may use at most 192 MiB of HBM per device.

```python
import math
import jax
import jax.numpy as jnp
from jax import lax

P_SIZE = 36
KL = 7
NPR = 4
NR = 128
NA = 128
NZ = 128


def draw_triple_cols(key, part):
    key = jax.random.fold_in(key, 11)
    raw_scores = jax.random.randint(key, (KL + 1, P_SIZE, P_SIZE), 0, 1 << 20)
    scores = raw_scores * P_SIZE + jnp.arange(P_SIZE, dtype=jnp.int32)
    diagonal = jnp.arange(P_SIZE, dtype=jnp.int32)[:, None] == jnp.arange(P_SIZE, dtype=jnp.int32)[None, :]
    leading = (jnp.arange(KL + 1, dtype=jnp.int32) == 0)[:, None, None]
    scores = jnp.where(leading & diagonal[None], -1, scores)
    ordering = jnp.argsort(scores, axis=-1)
    return ordering[:, :, :NPR].astype(jnp.int32)


def block_scale(rng, extent, cuts, smallest, top_value):
    factor_of, own = 1.0, jax.random.fold_in(rng, 6)
    for position, shards_of in cuts:
        steps = jnp.exp(jax.random.uniform(jax.random.fold_in(own, position), (shards_of,), jnp.float32, smallest / len(cuts), top_value / len(cuts)))
        factor_of = factor_of * jnp.repeat(steps, extent[position] // shards_of).reshape([-1 if axis == position else 1 for axis in range(len(extent))])
    return factor_of


def noise(stream_key, dims, spread, bound, shards=(), kind=jnp.bfloat16):
    gain = block_scale(stream_key, dims, shards, -0.22, 0.18) if shards else 1.0
    array = jax.random.normal(stream_key, dims, jnp.float32) * spread * gain
    return jnp.minimum(jnp.maximum(array, -bound), bound).astype(kind)


def setup_inputs(seed: int = 0) -> dict:
    arg_keys = jax.random.split(jax.random.key(seed), 6)
    return {
        "displacement": noise(arg_keys[0], (P_SIZE, 3, NA, NZ, NR), 1.0, 6.0, ((0, 2), (2, 4), (3, 32)), jnp.float32),
        "mean_modulus": jnp.clip(jnp.exp(math.log(2.0) - 1.3862944 * jax.random.uniform(arg_keys[1], (NA, NZ, NR), jnp.float32) ** block_scale(arg_keys[1], (NA, NZ, NR), ((0, 4), (1, 32)), -0.2, 0.2)), 0.5, 2.0),
        "kl_fields": noise(arg_keys[2], (KL, NA, NZ, NR), 0.3, 4.0, ((1, 4), (2, 32)), jnp.float32),
        "triple_cols": draw_triple_cols(jax.random.fold_in(arg_keys[5], 71), 0),
        "triple_vals": noise(arg_keys[4], (KL + 1, P_SIZE, NPR), 0.1, 1.5, (), jnp.float32),
    }


def coupling(slot_cols, slot_vals):
    modes = jnp.arange(slot_vals.shape[1], dtype=jnp.int32)
    matches = (slot_cols[..., None] == modes).astype(slot_vals.dtype)
    return jnp.sum(slot_vals[..., None] * matches, axis=2)


def lame_mix(dif_axial, dif_azim, dif_radial):
    component = jnp.arange(3, dtype=jnp.int32)[None, :, None, None, None]
    weight_axial = 1.0 + 2.0 * (component == 0).astype(dif_axial.dtype)
    weight_azim = 1.0 + 2.0 * (component == 1).astype(dif_axial.dtype)
    weight_radial = 1.0 + 2.0 * (component == 2).astype(dif_axial.dtype)
    return weight_axial * dif_axial + weight_azim * dif_azim + weight_radial * dif_radial


def stiffness(values):
    azim_up = jnp.roll(values, -1, axis=3)
    azim_down = jnp.roll(values, 1, axis=3)
    padded = jnp.pad(values, ((0, 0), (0, 0), (1, 1), (0, 0), (1, 1)))
    dif_axial = 2.0 * values - padded[:, :, 2:, :, 1:-1] - padded[:, :, :-2, :, 1:-1]
    dif_radial = 2.0 * values - padded[:, :, 1:-1, :, 2:] - padded[:, :, 1:-1, :, :-2]
    dif_azim = 2.0 * values - azim_up - azim_down
    return lame_mix(dif_axial, dif_azim, dif_radial)


def reference(displacement, mean_modulus, kl_fields, triple_cols, triple_vals):
    couple = coupling(triple_cols, triple_vals)
    fields = jnp.concatenate([mean_modulus[None], kl_fields], 0)
    stiffened = stiffness(displacement)

    def accumulate(running, inputs):
        matrix, factor = inputs
        product_part = jnp.einsum('ij,jcazr->icazr', matrix, stiffened, precision=lax.Precision.HIGHEST)
        return running + factor[None, None] * product_part, None

    running, unused = lax.scan(accumulate, jnp.zeros_like(stiffened), (couple, fields))
    return running
```

```python
import functools

import jax
import jax.numpy as jnp
from jax import lax
from jax.experimental import pallas as pl
from jax.experimental.pallas import tpu as pltpu
from jax.sharding import PartitionSpec as P

MESH = pl.DeviceIdType.MESH
F32 = jnp.float32
PAD = 8
IN_FLIGHT = 3


def place_of(group, place):
    if group == 0:
        return 1 + place // 2, 1 + place % 2
    if group == 1:
        return 1 + place // 2, 3 * (place % 2)
    return 3 * (place % 2), 2 * (group - 2) + place // 2


def kernel(
    shape,
    u_hbm, mean_hbm, kl_hbm, cols, vals, out_hbm,
    u, fields, azim_send, azim_recv, axial_send, axial_recv, stiff, work, out,
    load_sem, store_sem, azim_ssem, azim_rsem, axial_ssem, axial_rsem, send_sem, recv_sem,
):
    modes, comps, axials, azims, terms, slots = shape
    rows = axials * azims
    vectors = modes * comps
    chaos = lax.axis_index("chaos")
    azim = lax.axis_index("azim")
    axial = lax.axis_index("axial")
    n_azim, n_axial = lax.axis_size("azim"), lax.axis_size("axial")
    partner = {"chaos": 1 - chaos}
    azim_next = {"azim": lax.rem(azim + 1, n_azim)}
    azim_prev = {"azim": lax.rem(azim + n_azim - 1, n_azim)}
    axial_next = {"axial": lax.rem(axial + 1, n_axial)}
    axial_prev = {"axial": lax.rem(axial + n_axial - 1, n_axial)}
    has_prev, has_next = axial > 0, axial < n_axial - 1

    load_u = pltpu.make_async_copy(u_hbm, u.at[:, pl.ds(PAD, rows)], load_sem.at[0])
    load_mean = pltpu.make_async_copy(mean_hbm, fields.at[pl.ds(0, 1)], load_sem.at[1])
    load_kl = pltpu.make_async_copy(kl_hbm, fields.at[pl.ds(1, terms - 1)], load_sem.at[2])
    load_u.start()
    load_mean.start()
    load_kl.start()

    barrier = pltpu.get_barrier_semaphore()
    for target in (partner, azim_next, azim_prev, axial_next, axial_prev):
        pl.semaphore_signal(barrier, inc=1, device_id=target, device_id_type=MESH)

    def remote(source, target, ssem, rsem, device):
        return pltpu.make_async_remote_copy(
            src_ref=source, dst_ref=target, send_sem=ssem, recv_sem=rsem,
            device_id=device, device_id_type=MESH,
        )

    axial_copies = [
        remote(axial_send.at[s], axial_recv.at[s], axial_ssem.at[s], axial_rsem.at[s], d)
        for s, d in ((0, axial_prev), (1, axial_next))
    ]
    azim_copies = [
        remote(azim_send.at[s], azim_recv.at[s], azim_ssem.at[s], azim_rsem.at[s], d)
        for s, d in ((0, azim_prev), (1, azim_next))
    ]

    own = pl.ds(chaos * vectors, vectors)

    def exchange(n):
        part = stiff.at[n, own]
        return remote(part, part, send_sem.at[n], recv_sem.at[n], partner)

    load_u.wait()

    def pack_axial(p, carry):
        for s, first in ((0, PAD), (1, PAD + rows - azims)):
            axial_send[s, p, 0:azims, :] = u[2 * p, first:first + azims, :]
            axial_send[s, p, azims:2 * azims, :] = u[2 * p + 1, first:first + azims, :]
        return carry

    lax.fori_loop(0, vectors // 2, pack_axial, 0)
    pl.semaphore_wait(barrier, 5)

    @pl.when(has_prev)
    def _():
        axial_copies[0].start()

    @pl.when(has_next)
    def _():
        axial_copies[1].start()

    lane = lax.broadcasted_iota(jnp.int32, (8, 128), 1)
    first_lane, last_lane = lane == 0, lane == 127

    def stencil(group):
        where = [place_of(group, place) for place in range(4)]

        def body(j, carry):
            for c in range(comps):
                v = j * comps + c
                for place, (z, at) in enumerate(where):
                    base = PAD + at * 8 * azims + z

                    def layer(shift):
                        return u[v, pl.ds(base + shift, 8, stride=azims), :]

                    x = layer(0)
                    low = layer(-1) if z > 0 else azim_recv[1, v, at * 8:at * 8 + 8, :]
                    high = layer(1) if z < azims - 1 else azim_recv[0, v, at * 8:at * 8 + 8, :]
                    pairs = [
                        layer(azims) + layer(-azims),
                        low + high,
                        jnp.where(first_lane, 0.0, pltpu.roll(x, 1, 1))
                        + jnp.where(last_lane, 0.0, pltpu.roll(x, 127, 1)),
                    ]
                    total = pairs[(c + 1) % 3] + pairs[(c + 2) % 3] + 3.0 * pairs[c]
                    stiff[4 * group + place, chaos * vectors + v] = 10.0 * x - total
            return carry

        lax.fori_loop(0, modes, body, 0)

    def couple(group):
        def body(place, carry):
            n = 4 * group + place
            exchange(n).wait_recv()
            z, at = place_of(group, place)
            start = at * (8 * azims) + z
            blocks = pl.ds(start, 8, stride=azims)

            def gather(v, carry):
                work[v] = stiff[n, v]
                return carry

            lax.fori_loop(0, 2 * vectors, gather, 0, unroll=12)
            factors = [fields[k, blocks, :] for k in range(terms)]

            def row(i, carry):
                mode = chaos * modes + i
                total = [jnp.zeros((8, 128), F32) for c in range(comps)]
                for k in range(terms):
                    part = [None] * comps
                    for s in range(slots):
                        column, value = cols[k, s, mode] * comps, vals[k, s, mode]
                        for c in range(comps):
                            term = value * work[column + c]
                            part[c] = term if s == 0 else part[c] + term
                    for c in range(comps):
                        total[c] = total[c] + factors[k] * part[c]
                for c in range(comps):
                    out[i * comps + c, blocks, :] = total[c]
                return carry

            lax.fori_loop(0, modes, row, 0)
            exchange(n).wait_send()
            if group < 3:
                exchange(n + IN_FLIGHT).start()
            else:
                @pl.when(n + IN_FLIGHT < 16)
                def _():
                    exchange(n + IN_FLIGHT).start()

            return carry

        lax.fori_loop(0, 4, body, 0)

    def store(at):
        part = pl.ds(at * 8 * azims, 8 * azims)
        return pltpu.make_async_copy(out.at[:, part], out_hbm.at[:, part], store_sem.at[at])

    stencil(0)
    for n in range(IN_FLIGHT):
        exchange(n).start()

    def pack_azim(v, carry):
        for at in range(axials // 8):
            for s, z in ((0, 0), (1, azims - 1)):
                azim_send[s, v, at * 8:at * 8 + 8, :] = u[
                    v, pl.ds(PAD + at * 8 * azims + z, 8, stride=azims), :]
        return carry

    lax.fori_loop(0, vectors, pack_azim, 0, unroll=2)
    for copy in azim_copies:
        copy.start()

    for has, s, first in ((has_prev, 1, PAD - azims), (has_next, 0, PAD + rows)):
        @pl.when(has)
        def _(s=s, first=first):
            axial_copies[s].wait_recv()

            def unpack(p, carry):
                u[2 * p, first:first + azims, :] = axial_recv[s, p, 0:azims, :]
                u[2 * p + 1, first:first + azims, :] = axial_recv[s, p, azims:2 * azims, :]
                return carry

            lax.fori_loop(0, vectors // 2, unpack, 0)

        @pl.when(jnp.logical_not(has))
        def _(first=first):
            def clear(v, carry):
                u[v, first:first + azims, :] = jnp.zeros((azims, 128), F32)
                return carry

            lax.fori_loop(0, vectors, clear, 0)

    stencil(1)
    load_mean.wait()
    load_kl.wait()
    couple(0)
    for copy in azim_copies:
        copy.wait_recv()
    stencil(2)
    stencil(3)
    couple(1)
    couple(2)
    store(0).start()
    store(1).start()
    couple(3)
    store(2).start()
    store(3).start()

    @pl.when(has_prev)
    def _():
        axial_copies[0].wait_send()

    @pl.when(has_next)
    def _():
        axial_copies[1].wait_send()

    for copy in azim_copies:
        copy.wait_send()
    for at in range(4):
        store(at).wait()


def on_device(displacement, mean_modulus, kl_fields, triple_cols, triple_vals):
    modes, comps, axials, azims, radials = displacement.shape
    terms, all_modes, slots = triple_cols.shape
    vectors, rows = modes * comps, axials * azims
    dma = pltpu.SemaphoreType.DMA
    anywhere = pl.BlockSpec(memory_space=pl.ANY)
    scalar = pl.BlockSpec(memory_space=pltpu.SMEM)
    result = pl.pallas_call(
        functools.partial(kernel, (modes, comps, axials, azims, terms, slots)),
        out_shape=jax.ShapeDtypeStruct((vectors, rows, radials), F32),
        in_specs=[anywhere, anywhere, anywhere, scalar, scalar],
        out_specs=anywhere,
        scratch_shapes=[
            pltpu.VMEM((vectors, rows + 2 * PAD, radials), F32),
            pltpu.VMEM((terms, rows, radials), F32),
            pltpu.VMEM((2, vectors, axials, radials), F32),
            pltpu.VMEM((2, vectors, axials, radials), F32),
            pltpu.VMEM((2, vectors // 2, 2 * azims, radials), F32),
            pltpu.VMEM((2, vectors // 2, 2 * azims, radials), F32),
            pltpu.VMEM((16, 2 * vectors, 8, radials), F32),
            pltpu.VMEM((2 * vectors, 8, radials), F32),
            pltpu.VMEM((vectors, rows, radials), F32),
            dma((3,)), dma((4,)), dma((2,)), dma((2,)), dma((2,)), dma((2,)), dma((16,)), dma((16,)),
        ],
        compiler_params=pltpu.CompilerParams(
            collective_id=0, has_side_effects=True, vmem_limit_bytes=32 * 2**20
        ),
    )(
        displacement.reshape(vectors, rows, radials),
        mean_modulus.reshape(1, rows, radials),
        kl_fields.reshape(terms - 1, rows, radials),
        triple_cols.transpose(0, 2, 1),
        triple_vals.transpose(0, 2, 1),
    )
    return result.reshape(displacement.shape)


def solution(mesh):
    return jax.shard_map(
        on_device,
        mesh=mesh,
        in_specs=(
            P("chaos", None, "axial", "azim", None),
            P("axial", "azim", None),
            P(None, "axial", "azim", None),
            P(),
            P(),
        ),
        out_specs=P("chaos", None, "axial", "azim", None),
        check_vma=False,
    )
```

```python
import functools

import jax
import jax.numpy as jnp
from jax import lax
from jax.experimental import pallas as pl
from jax.experimental.pallas import tpu as pltpu
from jax.sharding import PartitionSpec as P

MESH = pl.DeviceIdType.MESH
F32 = jnp.float32
PAD = 8


def place_of(group, place):
    if group == 0:
        return 1 + place % 2, 1 + place // 2
    if group == 1:
        return 1 + place // 2, 3 * (place % 2)
    return 3 * (place % 2), 2 * (group - 2) + place // 2


LOADS = ((24, 48, 0, 1), (24, 48, 1, 2), (72, 32, 0, 3), (0, 24, 0, 3), (104, 24, 0, 3))


def kernel(
    shape,
    u_hbm, faces_hbm, mean_hbm, kl_hbm, cols_hbm, vals_hbm, out,
    u, fields, cols, vals, azim_send, azim_recv, axial_recv, stiff, work, matrix,
    load_sem, azim_ssem, azim_rsem, axial_ssem, axial_rsem, send_sem, recv_sem, hello,
):
    modes, comps, axials, azims, terms, slots = shape
    rows = axials * azims
    vectors = modes * comps
    last = 15
    chaos = lax.axis_index("chaos")
    azim = lax.axis_index("azim")
    axial = lax.axis_index("axial")
    n_azim, n_axial = lax.axis_size("azim"), lax.axis_size("axial")
    partner = {"chaos": 1 - chaos}
    azim_next = {"azim": lax.rem(azim + 1, n_azim)}
    azim_prev = {"azim": lax.rem(azim + n_azim - 1, n_azim)}
    axial_next = {"axial": lax.rem(axial + 1, n_axial)}
    axial_prev = {"axial": lax.rem(axial + n_axial - 1, n_axial)}
    has_prev, has_next = axial > 0, axial < n_axial - 1
    even = lax.rem(azim, 2) == 0

    barrier = pltpu.get_barrier_semaphore()
    for target in (partner, axial_next, axial_prev):
        pl.semaphore_signal(barrier, inc=1, device_id=target, device_id_type=MESH)

    @pl.when(even)
    def _():
        for target in (azim_next, azim_prev):
            pl.semaphore_signal(barrier, inc=1, device_id=target, device_id_type=MESH)

    loads = [
        pltpu.make_async_copy(
            u_hbm.at[:, pl.ds(c, count_c), pl.ds(first, count)],
            u.at[:, pl.ds(c, count_c), pl.ds(PAD + first, count)],
            load_sem.at[n],
        )
        for n, (first, count, c, count_c) in enumerate(LOADS)
    ]
    later = [
        pltpu.make_async_copy(source, target, load_sem.at[len(LOADS) + n])
        for n, (source, target) in enumerate((
            (mean_hbm, fields.at[pl.ds(0, 1)]),
            (kl_hbm, fields.at[pl.ds(1, terms - 1)]),
            (cols_hbm, cols),
            (vals_hbm, vals),
        ))
    ]
    for copy in loads + later:
        copy.start()

    def remote(source, target, ssem, rsem, device):
        return pltpu.make_async_remote_copy(
            src_ref=source, dst_ref=target, send_sem=ssem, recv_sem=rsem,
            device_id=device, device_id_type=MESH,
        )

    axial_copies = [
        remote(faces_hbm.at[:, :, a], axial_recv.at[s], axial_ssem.at[s], axial_rsem.at[s], d)
        for s, a, d in ((0, 0, axial_prev), (1, axials - 1, axial_next))
    ]
    azim_copies = [
        remote(azim_send.at[s], azim_recv.at[s], azim_ssem.at[s], azim_rsem.at[s], d)
        for s, d in ((0, azim_prev), (1, azim_next))
    ]

    own = pl.ds(chaos * modes, modes)
    first_own, first_other = chaos * modes, (1 - chaos) * modes

    def exchange(n, c):
        part = stiff.at[n, c, own]
        return remote(part, part, send_sem.at[n, c], recv_sem.at[n, c], partner)

    def exchange_block(n):
        part = stiff.at[n, :, own]
        return remote(part, part, send_sem.at[n, 0], recv_sem.at[n, 0], partner)

    lane = lax.broadcasted_iota(jnp.int32, (8, 128), 1)
    first_lane, last_lane = lane == 0, lane == 127

    def stencil(group, places, components):
        def body(j, carry):
            for c in components:
                for place in places:
                    z, at = place_of(group, place)
                    base = PAD + at * 8 * azims + z
                    face = pl.ds(at * 8, 8)

                    def layer(shift):
                        return u[j, c, pl.ds(base + shift, 8, stride=azims), :]

                    x = layer(0)
                    low = layer(-1) if z > 0 else azim_recv[1, j, c, face]
                    high = layer(1) if z < azims - 1 else azim_recv[0, j, c, face]
                    pairs = [
                        layer(azims) + layer(-azims),
                        low + high,
                        jnp.where(first_lane, 0.0, pltpu.roll(x, 1, 1))
                        + jnp.where(last_lane, 0.0, pltpu.roll(x, 127, 1)),
                    ]
                    total = pairs[(c + 1) % 3] + pairs[(c + 2) % 3] + 3.0 * pairs[c]
                    stiff[4 * group + place, c, first_own + j] = 10.0 * x - total
            return carry

        lax.fori_loop(0, modes, body, 0)

    def rows_of(group, place):
        z, at = place_of(group, place)
        return pl.ds(at * (8 * azims) + z, 8, stride=azims)

    def couple(cells, count, put):
        factors = [fields[k, cells, :] for k in range(terms)]

        def row(i, carry):
            mode = first_own + i
            total = [None] * count
            for k in range(terms):
                part = [None] * count
                for s in range(slots):
                    column, value = cols[k, s, mode], vals[k, s, mode]
                    for c in range(count):
                        term = value * work[c, column]
                        part[c] = term if s == 0 else part[c] + term
                for c in range(count):
                    scaled = factors[k] * part[c]
                    total[c] = scaled if k == 0 else total[c] + scaled
            for c in range(count):
                put(i, c, total[c])
            return carry

        lax.fori_loop(0, modes, row, 0)

    def finish(group, first, count, start):
        def block(place, carry):
            n = 4 * group + place
            cells = rows_of(group, place)

            exchange_block(n).wait_send()
            start(place)
            exchange_block(n).wait_recv()

            def gather(j, carry):
                for c in range(comps):
                    work[c, j] = stiff[n, c, j]
                return carry

            lax.fori_loop(0, 2 * modes, gather, 0, unroll=4)

            def put(i, c, value):
                out[i, c, cells, :] = value

            couple(cells, comps, put)
            return carry

        lax.fori_loop(first, first + count, block, 0)

    last_cells = rows_of(3, 3)
    zero = jnp.zeros((8, 128), F32)

    def begin_last():
        def gather(j, carry):
            for c in range(comps):
                work[c, first_own + j] = stiff[last, c, first_own + j]
                work[c, first_other + j] = zero
            return carry

        lax.fori_loop(0, modes, gather, 0, unroll=2)

        def put(i, c, value):
            out[i, c, last_cells, :] = value

        couple(last_cells, comps, put)

    def fill_matrix(first, count):
        def three(q, carry):
            def unit(j, carry):
                for c in range(comps):
                    work[c, j] = jnp.where(j == first_other + q * comps + c, zero + 1.0, zero)
                return carry

            lax.fori_loop(0, 2 * modes, unit, 0, unroll=4)

            def put(i, c, value):
                matrix[i, q * comps + c] = value

            couple(last_cells, comps, put)
            return carry

        lax.fori_loop(first, first + count, three, 0)

    def finish_last():
        def piece(c, carry):
            exchange(last, c).wait_recv()
            values = [stiff[last, c, first_other + j] for j in range(modes)]

            def row(i, carry):
                sums = [out[i, c, last_cells, :], zero, zero]
                for j in range(modes):
                    sums[j % 3] = sums[j % 3] + matrix[i, j] * values[j]
                out[i, c, last_cells, :] = sums[0] + (sums[1] + sums[2])
                return carry

            lax.fori_loop(0, modes, row, 0, unroll=2)
            return carry

        lax.fori_loop(0, comps, piece, 0)

    loads[0].wait()
    stencil(0, (0,), (0,))

    @pl.when(even)
    def _():
        pl.semaphore_wait(barrier, 3)

    @pl.when(jnp.logical_not(even))
    def _():
        pl.semaphore_wait(barrier, 5)

    @pl.when(has_prev)
    def _():
        axial_copies[0].start()

    @pl.when(has_next)
    def _():
        axial_copies[1].start()

    loads[1].wait()
    stencil(0, (0,), (1, 2))
    exchange_block(0).start()
    stencil(0, (1,), (0, 1, 2))
    exchange_block(1).start()

    @pl.when(jnp.logical_not(even))
    def _():
        for target in (azim_next, azim_prev):
            pl.semaphore_signal(hello, inc=1, device_id=target, device_id_type=MESH)

    for copy in loads[2:]:
        copy.wait()

    stencil(0, (2, 3), range(comps))

    for has, s, first in ((has_prev, 1, PAD - azims), (has_next, 0, PAD + rows)):
        @pl.when(has)
        def _(s=s, first=first):
            axial_copies[s].wait_recv()

            def unpack(j, carry):
                for c in range(comps):
                    u[j, c, first:first + azims, :] = axial_recv[s, j, c]
                return carry

            lax.fori_loop(0, modes, unpack, 0)

        @pl.when(jnp.logical_not(has))
        def _(first=first):
            def clear(j, carry):
                for c in range(comps):
                    u[j, c, first:first + azims, :] = jnp.zeros((azims, 128), F32)
                return carry

            lax.fori_loop(0, modes, clear, 0)

    stencil(1, range(4), range(comps))
    for copy in later:
        copy.wait()

    def two_on(group):
        return lambda place: exchange_block(4 * group + place + 2).start()

    finish(0, 0, 1, two_on(0))

    def pack_azim(j, carry):
        for c in range(comps):
            for at in range(axials // 8):
                for s, z in ((0, 0), (1, azims - 1)):
                    azim_send[s, j, c, pl.ds(at * 8, 8)] = u[
                        j, c, pl.ds(PAD + at * 8 * azims + z, 8, stride=azims), :]
        return carry

    lax.fori_loop(0, modes, pack_azim, 0)

    @pl.when(even)
    def _():
        pl.semaphore_wait(hello, 2)

    for copy in azim_copies:
        copy.start()

    finish(0, 1, 3, two_on(0))
    finish(1, 0, 2, two_on(1))
    for copy in azim_copies:
        copy.wait_recv()
    stencil(2, range(4), range(comps))
    stencil(3, range(4), range(comps))
    finish(1, 2, 2, two_on(1))
    begin_last()
    fill_matrix(0, 3)
    finish(2, 0, 4, two_on(2))
    fill_matrix(3, 3)

    def start_few(place):
        @pl.when(place == 0)
        def _():
            exchange_block(14).start()

        @pl.when(place == 2)
        def _():
            for c in range(comps):
                exchange(last, c).start()

    finish(3, 0, 3, start_few)
    finish_last()

    @pl.when(has_prev)
    def _():
        axial_copies[0].wait_send()

    @pl.when(has_next)
    def _():
        axial_copies[1].wait_send()

    for copy in azim_copies:
        copy.wait_send()
    for c in range(comps):
        exchange(last, c).wait_send()


def on_device(displacement, mean_modulus, kl_fields, triple_cols, triple_vals):
    modes, comps, axials, azims, radials = displacement.shape
    terms, all_modes, slots = triple_cols.shape
    rows = axials * azims
    dma = pltpu.SemaphoreType.DMA
    result = pl.pallas_call(
        functools.partial(kernel, (modes, comps, axials, azims, terms, slots)),
        out_shape=jax.ShapeDtypeStruct((modes, comps, rows, radials), F32),
        in_specs=[pl.BlockSpec(memory_space=pltpu.HBM)] * 6,
        out_specs=pl.BlockSpec(memory_space=pltpu.VMEM),
        scratch_shapes=[
            pltpu.VMEM((modes, comps, rows + 2 * PAD, radials), F32),
            pltpu.VMEM((terms, rows, radials), F32),
            pltpu.SMEM((terms, slots, all_modes), jnp.int32),
            pltpu.SMEM((terms, slots, all_modes), F32),
            pltpu.VMEM((2, modes, comps, axials, radials), F32),
            pltpu.VMEM((2, modes, comps, axials, radials), F32),
            pltpu.VMEM((2, modes, comps, azims, radials), F32),
            pltpu.VMEM((16, comps, 2 * modes, 8, radials), F32),
            pltpu.VMEM((comps, 2 * modes, 8, radials), F32),
            pltpu.VMEM((modes, modes, 8, radials), F32),
            dma((len(LOADS) + 4,)), dma((2,)), dma((2,)), dma((2,)), dma((2,)),
            dma((16, comps)), dma((16, comps)), pltpu.SemaphoreType.REGULAR,
        ],
        compiler_params=pltpu.CompilerParams(
            collective_id=0, has_side_effects=True, vmem_limit_bytes=32 * 2**20
        ),
    )(*(
        pltpu.with_memory_space_constraint(x, pltpu.HBM)
        for x in (
            displacement.reshape(modes, comps, rows, radials),
            displacement,
            mean_modulus.reshape(1, rows, radials),
            kl_fields.reshape(terms - 1, rows, radials),
            triple_cols.transpose(0, 2, 1),
            triple_vals.transpose(0, 2, 1),
        )
    ))
    return result.reshape(displacement.shape)


def solution(mesh):
    return jax.shard_map(
        on_device,
        mesh=mesh,
        in_specs=(
            P("chaos", None, "axial", "azim", None),
            P("axial", "azim", None),
            P(None, "axial", "azim", None),
            P(),
            P(),
        ),
        out_specs=P("chaos", None, "axial", "azim", None),
        check_vma=False,
    )
```

```python
import functools

import jax
import jax.numpy as jnp
from jax import lax
from jax.experimental import pallas as pl
from jax.experimental.pallas import tpu as pltpu
from jax.sharding import PartitionSpec as P

MESH = pl.DeviceIdType.MESH
F32 = jnp.float32
PAD = 8


def place_of(group, place):
    if group == 0:
        return 1 + place % 2, 1 + place // 2
    if group == 1:
        return 1 + place // 2, 3 * (place % 2)
    return 3 * (place % 2), 2 * (group - 2) + place // 2


LOADS = ((24, 48, 0, 1), (24, 48, 1, 2), (72, 32, 0, 3), (0, 24, 0, 3), (104, 24, 0, 3))


def kernel(
    shape,
    u_hbm, faces_hbm, mean_hbm, kl_hbm, cols_hbm, vals_hbm, out_any,
    u, fields, cols, vals, azim_send, azim_recv, axial_recv, stiff, work, matrix, out,
    load_sem, store_sem, azim_ssem, azim_rsem, axial_ssem, axial_rsem, send_sem, recv_sem, hello,
):
    modes, comps, axials, azims, terms, slots = shape
    rows = axials * azims
    vectors = modes * comps
    last = 15
    chaos = lax.axis_index("chaos")
    azim = lax.axis_index("azim")
    axial = lax.axis_index("axial")
    n_azim, n_axial = lax.axis_size("azim"), lax.axis_size("axial")
    partner = {"chaos": 1 - chaos}
    azim_next = {"azim": lax.rem(azim + 1, n_azim)}
    azim_prev = {"azim": lax.rem(azim + n_azim - 1, n_azim)}
    axial_next = {"axial": lax.rem(axial + 1, n_axial)}
    axial_prev = {"axial": lax.rem(axial + n_axial - 1, n_axial)}
    has_prev, has_next = axial > 0, axial < n_axial - 1
    even = lax.rem(azim, 2) == 0

    barrier = pltpu.get_barrier_semaphore()
    for target in (partner, axial_next, axial_prev):
        pl.semaphore_signal(barrier, inc=1, device_id=target, device_id_type=MESH)

    @pl.when(even)
    def _():
        for target in (azim_next, azim_prev):
            pl.semaphore_signal(barrier, inc=1, device_id=target, device_id_type=MESH)

    loads = [
        pltpu.make_async_copy(
            u_hbm.at[:, pl.ds(c, count_c), pl.ds(first, count)],
            u.at[:, pl.ds(c, count_c), pl.ds(PAD + first, count)],
            load_sem.at[min(n, 2)],
        )
        for n, (first, count, c, count_c) in enumerate(LOADS)
    ]
    later = [
        pltpu.make_async_copy(source, target, load_sem.at[max(3, 2 + n)])
        for n, (source, target) in enumerate((
            (mean_hbm, fields.at[pl.ds(0, 1), pl.ds(0, rows)]),
            (kl_hbm, fields.at[pl.ds(1, terms - 1), pl.ds(0, rows)]),
            (cols_hbm, cols),
            (vals_hbm, vals),
        ))
    ]
    for copy in loads[:3]:
        copy.start()

    def remote(source, target, ssem, rsem, device):
        return pltpu.make_async_remote_copy(
            src_ref=source, dst_ref=target, send_sem=ssem, recv_sem=rsem,
            device_id=device, device_id_type=MESH,
        )

    axial_copies = [
        remote(faces_hbm.at[:, :, a], axial_recv.at[s], axial_ssem.at[s], axial_rsem.at[s], d)
        for s, a, d in ((0, 0, axial_prev), (1, axials - 1, axial_next))
    ]
    azim_copies = [
        remote(azim_send.at[s], azim_recv.at[s], azim_ssem, azim_rsem.at[s], d)
        for s, d in ((0, azim_prev), (1, azim_next))
    ]

    own = pl.ds(chaos * modes, modes)
    first_own, first_other = chaos * modes, (1 - chaos) * modes

    def exchange(n, c):
        part = stiff.at[n, c, own]
        return remote(part, part, send_sem, recv_sem.at[n if n == 0 else n + c], partner)

    def exchange_block(n):
        part = stiff.at[n, :, own]
        return remote(part, part, send_sem, recv_sem.at[n], partner)

    lane = lax.broadcasted_iota(jnp.int32, (8, 128), 1)
    first_lane, last_lane = lane == 0, lane == 127

    def stencil(group, places, unroll, components=(0, 1, 2)):
        def body(j, carry):
            for c in components:
                for place in places:
                    z, at = place_of(group, place)
                    base = PAD + at * 8 * azims + z
                    face = pl.ds(at * 8, 8)

                    def layer(shift):
                        return u[j, c, pl.ds(base + shift, 8, stride=azims), :]

                    x = layer(0)
                    low = layer(-1) if z > 0 else azim_recv[1, j, c, face]
                    high = layer(1) if z < azims - 1 else azim_recv[0, j, c, face]
                    pairs = [
                        layer(azims) + layer(-azims),
                        low + high,
                        jnp.where(first_lane, 0.0, pltpu.roll(x, 1, 1))
                        + jnp.where(last_lane, 0.0, pltpu.roll(x, 127, 1)),
                    ]
                    total = pairs[(c + 1) % 3] + pairs[(c + 2) % 3] + 3.0 * pairs[c]
                    stiff[4 * group + place, c, first_own + j] = 10.0 * x - total
            return carry

        lax.fori_loop(0, modes, body, 0, unroll=unroll)

    def rows_of(group, place):
        z, at = place_of(group, place)
        return pl.ds(at * (8 * azims) + z, 8, stride=azims)

    def couple(cells, count, put):
        factors = [fields[k, cells, :] for k in range(terms)]

        def row(i, carry):
            mode = first_own + i
            total = [None] * count
            for k in range(terms):
                part = [None] * count
                for s in range(slots):
                    column, value = cols[k, s, mode], vals[k, s, mode]
                    for c in range(count):
                        term = value * work[c, column]
                        part[c] = term if s == 0 else part[c] + term
                for c in range(count):
                    scaled = factors[k] * part[c]
                    total[c] = scaled if k == 0 else total[c] + scaled
            for c in range(count):
                put(i, c, total[c])
            return carry

        lax.fori_loop(0, modes, row, 0)

    def finish(group, first, count):
        def block(place, carry):
            n = 4 * group + place
            cells = rows_of(group, place)

            exchange_block(n).wait_recv()

            def gather(j, carry):
                for c in range(comps):
                    work[c, j] = stiff[n, c, j]
                return carry

            lax.fori_loop(0, 2 * modes, gather, 0, unroll=4)

            def put(i, c, value):
                out[i, c, cells, :] = value

            couple(cells, comps, put)
            return carry

        lax.fori_loop(first, first + count, block, 0)

    last_cells = rows_of(3, 3)
    zero = jnp.zeros((8, 128), F32)

    def begin_last():
        def gather(j, carry):
            for c in range(comps):
                work[c, first_own + j] = stiff[last, c, first_own + j]
                work[c, first_other + j] = zero
            return carry

        lax.fori_loop(0, modes, gather, 0, unroll=2)

        def put(i, c, value):
            out[i, c, last_cells, :] = value

        couple(last_cells, comps, put)

    def fill_matrix(first, count):
        def three(q, carry):
            def unit(j, carry):
                for c in range(comps):
                    work[c, j] = jnp.where(j == first_other + q * comps + c, zero + 1.0, zero)
                return carry

            lax.fori_loop(0, 2 * modes, unit, 0, unroll=4)

            def put(i, c, value):
                matrix[i, q * comps + c] = value

            couple(last_cells, comps, put)
            return carry

        lax.fori_loop(first, first + count, three, 0)

    def store(at, c):
        part = pl.ds(at * 8 * azims, 8 * azims)
        return pltpu.make_async_copy(out.at[:, c, part], out_any.at[:, c, part], store_sem)

    def finish_last():
        def piece(c, carry):
            exchange(last, c).wait_recv()
            values = [stiff[last, c, first_other + j] for j in range(modes)]

            def row(i, carry):
                sums = [out[i, c, last_cells, :], zero, zero]
                for j in range(modes):
                    sums[j % 3] = sums[j % 3] + matrix[i, j] * values[j]
                out[i, c, last_cells, :] = sums[0] + (sums[1] + sums[2])
                return carry

            lax.fori_loop(0, modes, row, 0, unroll=3)
            store(3, c).start()
            return carry

        lax.fori_loop(0, comps, piece, 0)

    loads[0].wait()
    stencil(0, (0,), 18, (0,))

    @pl.when(even)
    def _():
        pl.semaphore_wait(barrier, 3)

    @pl.when(jnp.logical_not(even))
    def _():
        pl.semaphore_wait(barrier, 5)

    @pl.when(has_prev)
    def _():
        axial_copies[0].start()

    @pl.when(has_next)
    def _():
        axial_copies[1].start()

    for copy in loads[3:] + later:
        copy.start()
    exchange(0, 0).start()
    loads[1].wait()
    stencil(0, (0,), 9, (1, 2))
    exchange(0, 1).start()
    exchange(0, 2).start()

    @pl.when(jnp.logical_not(even))
    def _():
        for target in (azim_next, azim_prev):
            pl.semaphore_signal(hello, inc=1, device_id=target, device_id_type=MESH)

    stencil(0, (1,), 6)
    exchange_block(1).start()
    rest = sum(count for first, count, c, count_c in LOADS[2:])
    pltpu.make_async_copy(
        u_hbm.at[:, :, pl.ds(0, rest)], u.at[:, :, pl.ds(PAD, rest)], load_sem.at[2]
    ).wait()
    stencil(0, (2, 3), 3)
    exchange_block(2).start()
    exchange_block(3).start()

    def pack_azim(j, carry):
        for c in range(comps):
            for at in range(axials // 8):
                for s, z in ((0, 0), (1, azims - 1)):
                    azim_send[s, j, c, pl.ds(at * 8, 8)] = u[
                        j, c, pl.ds(PAD + at * 8 * azims + z, 8, stride=azims), :]
        return carry

    lax.fori_loop(0, modes, pack_azim, 0)

    for has, s, first in ((has_prev, 1, PAD - azims), (has_next, 0, PAD + rows)):
        @pl.when(has)
        def _(s=s, first=first):
            axial_copies[s].wait_recv()

            def unpack(j, carry):
                for c in range(comps):
                    u[j, c, first:first + azims, :] = axial_recv[s, j, c]
                return carry

            lax.fori_loop(0, modes, unpack, 0, unroll=3)

        @pl.when(jnp.logical_not(has))
        def _(first=first):
            def clear(j, carry):
                for c in range(comps):
                    u[j, c, first:first + azims, :] = jnp.zeros((azims, 128), F32)
                return carry

            lax.fori_loop(0, modes, clear, 0, unroll=3)

    stencil(1, range(4), 2)
    for n in range(4, 8):
        exchange_block(n).start()

    @pl.when(even)
    def _():
        pl.semaphore_wait(hello, 2)

    for copy in azim_copies:
        copy.start()
    whole = fields.at[:, pl.ds(0, rows)]
    pltpu.make_async_copy(whole, whole, load_sem.at[3]).wait()
    for copy in later[2:]:
        copy.wait()
    finish(0, 0, 4)
    finish(1, 0, 1)
    for copy in azim_copies:
        copy.wait_recv()
    stencil(2, range(4), 2)
    for n in range(8, 12):
        exchange_block(n).start()
    stencil(3, range(4), 2)
    for n in range(12, last):
        exchange_block(n).start()
    for c in range(comps):
        exchange(last, c).start()
    finish(1, 1, 3)
    begin_last()
    fill_matrix(0, 3)
    finish(2, 0, 4)
    for at in range(2):
        for c in range(comps):
            store(at, c).start()
    fill_matrix(3, 3)

    finish(3, 0, 2)
    for c in range(comps):
        store(2, c).start()
    finish(3, 2, 1)
    finish_last()

    @pl.when(has_prev)
    def _():
        axial_copies[0].wait_send()

    @pl.when(has_next)
    def _():
        axial_copies[1].wait_send()

    remote(azim_send, azim_recv, azim_ssem, azim_rsem.at[0], azim_next).wait_send()
    every = stiff.at[:, :, own]
    remote(every, every, send_sem, recv_sem.at[0], partner).wait_send()
    pltpu.make_async_copy(out.at[:, :, pl.ds(0, rows)], out_any, store_sem).wait()


def on_device(displacement, mean_modulus, kl_fields, triple_cols, triple_vals):
    modes, comps, axials, azims, radials = displacement.shape
    terms, all_modes, slots = triple_cols.shape
    rows = axials * azims
    dma = pltpu.SemaphoreType.DMA
    result = pl.pallas_call(
        functools.partial(kernel, (modes, comps, axials, azims, terms, slots)),
        out_shape=jax.ShapeDtypeStruct((modes, comps, rows, radials), F32),
        in_specs=[pl.BlockSpec(memory_space=pltpu.HBM)] * 6,
        out_specs=pl.BlockSpec(memory_space=pl.ANY),
        scratch_shapes=[
            pltpu.VMEM((modes, comps, rows + 2 * PAD, radials), F32),
            pltpu.VMEM((terms, rows + PAD, radials), F32),
            pltpu.SMEM((terms, slots, all_modes), jnp.int32),
            pltpu.SMEM((terms, slots, all_modes), F32),
            pltpu.VMEM((2, modes, comps, axials, radials), F32),
            pltpu.VMEM((2, modes, comps, axials, radials), F32),
            pltpu.VMEM((2, modes, comps, azims, radials), F32),
            pltpu.VMEM((16, comps, 2 * modes, 8, radials), F32),
            pltpu.VMEM((comps, 2 * modes, 8, radials), F32),
            pltpu.VMEM((modes, modes, 8, radials), F32),
            pltpu.VMEM((modes, comps, rows + PAD, radials), F32),
            dma((6,)), dma(()), dma(()), dma((2,)), dma((2,)), dma((2,)),
            dma(()), dma((18,)), pltpu.SemaphoreType.REGULAR,
        ],
        compiler_params=pltpu.CompilerParams(
            collective_id=0, has_side_effects=True, vmem_limit_bytes=32 * 2**20
        ),
    )(*(
        pltpu.with_memory_space_constraint(x, pltpu.HBM)
        for x in (
            displacement.reshape(modes, comps, rows, radials),
            displacement,
            mean_modulus.reshape(1, rows, radials),
            kl_fields.reshape(terms - 1, rows, radials),
            triple_cols.transpose(0, 2, 1),
            triple_vals.transpose(0, 2, 1),
        )
    ))
    return result.reshape(displacement.shape)


def solution(mesh):
    return jax.shard_map(
        on_device,
        mesh=mesh,
        in_specs=(
            P("chaos", None, "axial", "azim", None),
            P("axial", "azim", None),
            P(None, "axial", "azim", None),
            P(),
            P(),
        ),
        out_specs=P("chaos", None, "axial", "azim", None),
        check_vma=False,
    )
```

```python
import functools

import jax
import jax.numpy as jnp
from jax import lax
from jax.experimental import pallas as pl
from jax.experimental.pallas import tpu as pltpu
from jax.sharding import PartitionSpec as P

MESH = pl.DeviceIdType.MESH
F32 = jnp.float32
PAD = 8


def place_of(group, place):
    if group == 0:
        return 1 + place % 2, 1 + place // 2
    if group == 1:
        return 1 + place // 2, 3 * (place % 2)
    return 3 * (place % 2), 2 * (group - 2) + place // 2


FEW = 6
TAIL = ((0, 9), (9, 6), (15, 3))
LOADS = (
    (0, FEW, 0, 1, 24, 48), (FEW, 12, 0, 1, 24, 48), (0, 18, 1, 2, 24, 48),
    (0, 18, 0, 3, 72, 32), (0, 18, 0, 3, 0, 24), (0, 18, 0, 3, 104, 24),
)


def kernel(
    shape,
    u_hbm, faces_hbm, mean_hbm, kl_hbm, cols_hbm, vals_hbm, out_any,
    u, fields, cols, vals, azim_send, azim_recv, axial_recv, stiff, work, matrix, out,
    load_sem, store_sem, azim_ssem, azim_rsem, axial_ssem, axial_rsem, send_sem, recv_sem, hello,
):
    modes, comps, axials, azims, terms, slots = shape
    rows = axials * azims
    vectors = modes * comps
    last = 15
    chaos = lax.axis_index("chaos")
    azim = lax.axis_index("azim")
    axial = lax.axis_index("axial")
    n_azim, n_axial = lax.axis_size("azim"), lax.axis_size("axial")
    partner = {"chaos": 1 - chaos}
    azim_next = {"azim": lax.rem(azim + 1, n_azim)}
    azim_prev = {"azim": lax.rem(azim + n_azim - 1, n_azim)}
    axial_next = {"axial": lax.rem(axial + 1, n_axial)}
    axial_prev = {"axial": lax.rem(axial + n_axial - 1, n_axial)}
    has_prev, has_next = axial > 0, axial < n_axial - 1
    even = lax.rem(azim, 2) == 0

    loads = [
        pltpu.make_async_copy(
            u_hbm.at[pl.ds(j, count_j), pl.ds(c, count_c), pl.ds(first, count)],
            u.at[pl.ds(j, count_j), pl.ds(c, count_c), pl.ds(PAD + first, count)],
            load_sem.at[min(n, 3)],
        )
        for n, (j, count_j, c, count_c, first, count) in enumerate(LOADS)
    ]
    loads[0].start()

    barrier = pltpu.get_barrier_semaphore()
    for target in (partner, axial_next, axial_prev):
        pl.semaphore_signal(barrier, inc=1, device_id=target, device_id_type=MESH)

    @pl.when(even)
    def _():
        for target in (azim_next, azim_prev):
            pl.semaphore_signal(barrier, inc=1, device_id=target, device_id_type=MESH)

    later = [
        pltpu.make_async_copy(source, target, load_sem.at[max(4, 3 + n)])
        for n, (source, target) in enumerate((
            (mean_hbm, fields.at[pl.ds(0, 1), pl.ds(0, rows)]),
            (kl_hbm, fields.at[pl.ds(1, terms - 1), pl.ds(0, rows)]),
            (cols_hbm, cols),
            (vals_hbm, vals),
        ))
    ]
    for copy in loads[1:4]:
        copy.start()

    def remote(source, target, ssem, rsem, device):
        return pltpu.make_async_remote_copy(
            src_ref=source, dst_ref=target, send_sem=ssem, recv_sem=rsem,
            device_id=device, device_id_type=MESH,
        )

    axial_copies = [
        remote(faces_hbm.at[:, :, a], axial_recv.at[s], axial_ssem.at[s], axial_rsem.at[s], d)
        for s, a, d in ((0, 0, axial_prev), (1, axials - 1, axial_next))
    ]
    azim_copies = [
        remote(azim_send.at[s], azim_recv.at[s], azim_ssem, azim_rsem.at[s], d)
        for s, d in ((0, azim_prev), (1, azim_next))
    ]

    first_own, first_other = chaos * modes, (1 - chaos) * modes

    def exchange(n, c):
        part = stiff.at[n, chaos, c]
        return remote(part, part, send_sem, recv_sem.at[n if n == 0 else n + c], partner)

    def exchange_some(n, c, j, count, sem):
        part = stiff.at[n, chaos, c, pl.ds(j, count)]
        return remote(part, part, send_sem, recv_sem.at[sem], partner)

    def exchange_tail(n):
        return exchange_some(last, comps - 1, *TAIL[n], last + comps - 1 + n)

    def exchange_block(n):
        part = stiff.at[n, chaos]
        return remote(part, part, send_sem, recv_sem.at[n], partner)

    lane = lax.broadcasted_iota(jnp.int32, (8, 128), 1)
    first_lane, last_lane = lane == 0, lane == 127

    def stencil(group, places, unroll, components=(0, 1, 2), span=(0, modes)):
        def body(j, carry):
            for c in components:
                for place in places:
                    z, at = place_of(group, place)
                    base = PAD + at * 8 * azims + z
                    face = pl.ds(at * 8, 8)

                    def layer(shift):
                        return u[j, c, pl.ds(base + shift, 8, stride=azims), :]

                    x = layer(0)
                    low = layer(-1) if z > 0 else azim_recv[1, j, c, face]
                    high = layer(1) if z < azims - 1 else azim_recv[0, j, c, face]
                    pairs = [
                        layer(azims) + layer(-azims),
                        low + high,
                        jnp.where(first_lane, 0.0, pltpu.roll(x, 1, 1))
                        + jnp.where(last_lane, 0.0, pltpu.roll(x, 127, 1)),
                    ]
                    total = pairs[(c + 1) % 3] + pairs[(c + 2) % 3] + 3.0 * pairs[c]
                    stiff[4 * group + place, chaos, c, j] = 10.0 * x - total
            return carry

        lax.fori_loop(*span, body, 0, unroll=unroll)

    def rows_of(group, place):
        z, at = place_of(group, place)
        return pl.ds(at * (8 * azims) + z, 8, stride=azims)

    def couple(cells, count, put):
        factors = [fields[k, cells, :] for k in range(terms)]

        def row(i, carry):
            mode = first_own + i
            total = [None] * count
            for k in range(terms):
                part = [None] * count
                for s in range(slots):
                    column, value = cols[k, s, mode], vals[k, s, mode]
                    for c in range(count):
                        term = value * work[c, column]
                        part[c] = term if s == 0 else part[c] + term
                for c in range(count):
                    scaled = factors[k] * part[c]
                    total[c] = scaled if k == 0 else total[c] + scaled
            for c in range(count):
                put(i, c, total[c])
            return carry

        lax.fori_loop(0, modes, row, 0)

    def finish(group, first, count):
        def block(place, carry):
            n = 4 * group + place
            cells = rows_of(group, place)

            exchange_block(n).wait_recv()

            def gather(j, carry):
                for half in range(2):
                    for c in range(comps):
                        work[c, half * modes + j] = stiff[n, half, c, j]
                return carry

            lax.fori_loop(0, modes, gather, 0, unroll=3)

            def put(i, c, value):
                out[i, c, cells, :] = value

            couple(cells, comps, put)
            return carry

        lax.fori_loop(first, first + count, block, 0)

    last_cells = rows_of(3, 3)
    zero = jnp.zeros((8, 128), F32)

    def begin_last():
        def gather(j, carry):
            for c in range(comps):
                work[c, first_own + j] = stiff[last, chaos, c, j]
                work[c, first_other + j] = zero
            return carry

        lax.fori_loop(0, modes, gather, 0, unroll=2)

        def put(i, c, value):
            out[i, c, last_cells, :] = value

        couple(last_cells, comps, put)

    def fill_matrix(first, count):
        def three(q, carry):
            def unit(j, carry):
                for c in range(comps):
                    work[c, j] = jnp.where(j == first_other + q * comps + c, zero + 1.0, zero)
                return carry

            lax.fori_loop(0, 2 * modes, unit, 0, unroll=4)

            def put(i, c, value):
                matrix[i, q * comps + c] = value

            couple(last_cells, comps, put)
            return carry

        lax.fori_loop(first, first + count, three, 0)

    def store(at, c):
        part = pl.ds(at * 8 * azims, 8 * azims)
        return pltpu.make_async_copy(out.at[:, c, part], out_any.at[:, c, part], store_sem)

    def finish_last():
        def take(c, first, count, unroll):
            values = [stiff[last, 1 - chaos, c, first + j] for j in range(count)]

            def row(i, carry):
                sums = [out[i, c, last_cells, :], zero, zero]
                for j in range(count):
                    sums[j % 3] = sums[j % 3] + matrix[i, first + j] * values[j]
                out[i, c, last_cells, :] = sums[0] + (sums[1] + sums[2])
                return carry

            lax.fori_loop(0, modes, row, 0, unroll=unroll)

        def piece(c, carry):
            exchange(last, c).wait_recv()
            take(c, 0, modes, 3)
            store(3, c).start()
            return carry

        lax.fori_loop(0, comps - 1, piece, 0)
        for n, (first, count) in enumerate(TAIL):
            exchange_tail(n).wait_recv()
            take(comps - 1, first, count, 18 // count)
        store(3, comps - 1).start()

    @pl.when(even)
    def _():
        pl.semaphore_wait(barrier, 3)

    @pl.when(jnp.logical_not(even))
    def _():
        pl.semaphore_wait(barrier, 5)

    @pl.when(has_prev)
    def _():
        axial_copies[0].start()

    @pl.when(has_next)
    def _():
        axial_copies[1].start()

    for copy in loads[4:] + later:
        copy.start()
    loads[0].wait()
    stencil(0, (0,), FEW, (0,), (0, FEW))
    exchange_some(0, 0, 0, FEW, 0).start()
    loads[1].wait()
    stencil(0, (0,), modes - FEW, (0,), (FEW, modes))
    exchange_some(0, 0, FEW, modes - FEW, 0).start()
    loads[2].wait()
    stencil(0, (0,), 9, (1, 2))
    exchange(0, 1).start()
    exchange(0, 2).start()

    @pl.when(jnp.logical_not(even))
    def _():
        for target in (azim_next, azim_prev):
            pl.semaphore_signal(hello, inc=1, device_id=target, device_id_type=MESH)

    stencil(0, (1,), 6)
    exchange_block(1).start()
    rest = sum(load[-1] for load in LOADS[3:])
    pltpu.make_async_copy(
        u_hbm.at[:, :, pl.ds(0, rest)], u.at[:, :, pl.ds(PAD, rest)], load_sem.at[3]
    ).wait()
    stencil(0, (2, 3), 3)
    exchange_block(2).start()
    exchange_block(3).start()

    def pack_azim(j, carry):
        for c in range(comps):
            for at in range(axials // 8):
                for s, z in ((0, 0), (1, azims - 1)):
                    azim_send[s, j, c, pl.ds(at * 8, 8)] = u[
                        j, c, pl.ds(PAD + at * 8 * azims + z, 8, stride=azims), :]
        return carry

    lax.fori_loop(0, modes, pack_azim, 0)

    for has, s, first in ((has_prev, 1, PAD - azims), (has_next, 0, PAD + rows)):
        @pl.when(has)
        def _(s=s, first=first):
            axial_copies[s].wait_recv()

            def unpack(j, carry):
                for c in range(comps):
                    u[j, c, first:first + azims, :] = axial_recv[s, j, c]
                return carry

            lax.fori_loop(0, modes, unpack, 0, unroll=3)

        @pl.when(jnp.logical_not(has))
        def _(first=first):
            def clear(j, carry):
                for c in range(comps):
                    u[j, c, first:first + azims, :] = jnp.zeros((azims, 128), F32)
                return carry

            lax.fori_loop(0, modes, clear, 0, unroll=3)

    stencil(1, range(4), 2)
    for n in range(4, 8):
        exchange_block(n).start()

    @pl.when(even)
    def _():
        pl.semaphore_wait(hello, 2)

    for copy in azim_copies:
        copy.start()
    whole = fields.at[:, pl.ds(0, rows)]
    pltpu.make_async_copy(whole, whole, load_sem.at[4]).wait()
    for copy in later[2:]:
        copy.wait()
    finish(0, 0, 4)
    finish(1, 0, 1)
    for copy in azim_copies:
        copy.wait_recv()
    stencil(2, range(4), 2)
    for n in range(8, 12):
        exchange_block(n).start()
    stencil(3, range(4), 2)
    for n in range(12, last):
        exchange_block(n).start()
    for c in range(comps - 1):
        exchange(last, c).start()
    for n in range(len(TAIL)):
        exchange_tail(n).start()
    finish(1, 1, 3)
    begin_last()
    fill_matrix(0, 3)
    finish(2, 0, 4)
    for at in range(2):
        for c in range(comps):
            store(at, c).start()
    fill_matrix(3, 3)

    finish(3, 0, 2)
    for c in range(comps):
        store(2, c).start()
    finish(3, 2, 1)
    finish_last()

    @pl.when(has_prev)
    def _():
        axial_copies[0].wait_send()

    @pl.when(has_next)
    def _():
        axial_copies[1].wait_send()

    remote(azim_send, azim_recv, azim_ssem, azim_rsem.at[0], azim_next).wait_send()
    every = stiff.at[:, chaos]
    remote(every, every, send_sem, recv_sem.at[0], partner).wait_send()
    pltpu.make_async_copy(out.at[:, :, pl.ds(0, rows)], out_any, store_sem).wait()


def on_device(displacement, mean_modulus, kl_fields, triple_cols, triple_vals):
    modes, comps, axials, azims, radials = displacement.shape
    terms, all_modes, slots = triple_cols.shape
    rows = axials * azims
    dma = pltpu.SemaphoreType.DMA
    result = pl.pallas_call(
        functools.partial(kernel, (modes, comps, axials, azims, terms, slots)),
        out_shape=jax.ShapeDtypeStruct((modes, comps, rows, radials), F32),
        in_specs=[pl.BlockSpec(memory_space=pltpu.HBM)] * 6,
        out_specs=pl.BlockSpec(memory_space=pl.ANY),
        scratch_shapes=[
            pltpu.VMEM((modes, comps, rows + 2 * PAD, radials), F32),
            pltpu.VMEM((terms, rows + PAD, radials), F32),
            pltpu.SMEM((terms, slots, all_modes), jnp.int32),
            pltpu.SMEM((terms, slots, all_modes), F32),
            pltpu.VMEM((2, modes, comps, axials, radials), F32),
            pltpu.VMEM((2, modes, comps, axials, radials), F32),
            pltpu.VMEM((2, modes, comps, azims, radials), F32),
            pltpu.VMEM((16, 2, comps, modes, 8, radials), F32),
            pltpu.VMEM((comps, 2 * modes, 8, radials), F32),
            pltpu.VMEM((modes, modes, 8, radials), F32),
            pltpu.VMEM((modes, comps, rows + PAD, radials), F32),
            dma((7,)), dma(()), dma(()), dma((2,)), dma((2,)), dma((2,)),
            dma(()), dma((20,)), pltpu.SemaphoreType.REGULAR,
        ],
        compiler_params=pltpu.CompilerParams(
            collective_id=0, has_side_effects=True, vmem_limit_bytes=32 * 2**20
        ),
    )(*(
        pltpu.with_memory_space_constraint(x, pltpu.HBM)
        for x in (
            displacement.reshape(modes, comps, rows, radials),
            displacement,
            mean_modulus.reshape(1, rows, radials),
            kl_fields.reshape(terms - 1, rows, radials),
            triple_cols.transpose(0, 2, 1),
            triple_vals.transpose(0, 2, 1),
        )
    ))
    return result.reshape(displacement.shape)


def solution(mesh):
    return jax.shard_map(
        on_device,
        mesh=mesh,
        in_specs=(
            P("chaos", None, "axial", "azim", None),
            P("axial", "azim", None),
            P(None, "axial", "azim", None),
            P(),
            P(),
        ),
        out_specs=P("chaos", None, "axial", "azim", None),
        check_vma=False,
    )
```

```python
import functools

import jax
import jax.numpy as jnp
from jax import lax
from jax.experimental import pallas as pl
from jax.experimental.pallas import tpu as pltpu
from jax.sharding import PartitionSpec as P

MESH = pl.DeviceIdType.MESH
F32 = jnp.float32
PAD = 8


def place_of(group, place):
    if group == 0:
        return 1 + place % 2, 1 + place // 2
    if group == 1:
        return 1 + place // 2, 3 * (place % 2)
    return 3 * (place % 2), 2 * (group - 2) + place // 2


FEW = 6
TAIL = ((0, 9), (9, 6), (15, 3))
LOADS = (
    (0, FEW, 0, 1, 24, 48), (FEW, 12, 0, 1, 24, 48), (0, 18, 1, 2, 24, 48),
    (0, 18, 0, 3, 72, 32), (0, 18, 0, 3, 0, 24), (0, 18, 0, 3, 104, 24),
)


def kernel(
    shape,
    u_hbm, faces_hbm, mean_hbm, kl_hbm, cols_hbm, vals_hbm, out_any,
    u, fields, cols, vals, azim_send, azim_recv, axial_recv, stiff, work, matrix, out,
    load_sem, store_sem, azim_ssem, azim_rsem, axial_ssem, axial_rsem, send_sem, recv_sem, hello,
):
    modes, comps, axials, azims, terms, slots = shape
    rows = axials * azims
    vectors = modes * comps
    last = 15
    chaos = lax.axis_index("chaos")
    azim = lax.axis_index("azim")
    axial = lax.axis_index("axial")
    n_azim, n_axial = lax.axis_size("azim"), lax.axis_size("axial")
    partner = {"chaos": 1 - chaos}
    azim_next = {"azim": lax.rem(azim + 1, n_azim)}
    azim_prev = {"azim": lax.rem(azim + n_azim - 1, n_azim)}
    axial_next = {"axial": lax.rem(axial + 1, n_axial)}
    axial_prev = {"axial": lax.rem(axial + n_axial - 1, n_axial)}
    has_prev, has_next = axial > 0, axial < n_axial - 1
    even = lax.rem(azim, 2) == 0
    odd = jnp.logical_not(even)
    half = n_azim // 2
    second = chaos == 1
    cut_before = jnp.logical_and(second, azim == half - 1)
    cut_after = jnp.logical_and(second, azim == half)
    relays = jnp.logical_and(chaos == 0, azim == half)

    loads = [
        pltpu.make_async_copy(
            u_hbm.at[pl.ds(j, count_j), pl.ds(c, count_c), pl.ds(first, count)],
            u.at[pl.ds(j, count_j), pl.ds(c, count_c), pl.ds(PAD + first, count)],
            load_sem.at[min(n, 3)],
        )
        for n, (j, count_j, c, count_c, first, count) in enumerate(LOADS)
    ]
    loads[0].start()

    barrier = pltpu.get_barrier_semaphore()
    for target in (partner, axial_next, axial_prev):
        pl.semaphore_signal(barrier, inc=1, device_id=target, device_id_type=MESH)

    @pl.when(even)
    def _():
        pl.semaphore_signal(barrier, inc=1, device_id=azim_next, device_id_type=MESH)

    @pl.when(jnp.logical_and(even, jnp.logical_not(cut_after)))
    def _():
        pl.semaphore_signal(barrier, inc=1, device_id=azim_prev, device_id_type=MESH)

    later = [
        pltpu.make_async_copy(source, target, load_sem.at[max(4, 3 + n)])
        for n, (source, target) in enumerate((
            (mean_hbm, fields.at[pl.ds(0, 1), pl.ds(0, rows)]),
            (kl_hbm, fields.at[pl.ds(1, terms - 1), pl.ds(0, rows)]),
            (cols_hbm, cols),
            (vals_hbm, vals),
        ))
    ]
    for copy in loads[1:4]:
        copy.start()

    def remote(source, target, ssem, rsem, device):
        return pltpu.make_async_remote_copy(
            src_ref=source, dst_ref=target, send_sem=ssem, recv_sem=rsem,
            device_id=device, device_id_type=MESH,
        )

    axial_copies = [
        remote(faces_hbm.at[:, :, a], axial_recv.at[s], axial_ssem.at[s], axial_rsem.at[s], d)
        for s, a, d in ((0, 0, axial_prev), (1, axials - 1, axial_next))
    ]
    azim_copies = [
        remote(azim_send.at[s], azim_recv.at[s], azim_ssem, azim_rsem.at[s], d)
        for s, d in ((0, azim_prev), (1, azim_next))
    ]

    first_own, first_other = chaos * modes, (1 - chaos) * modes

    def exchange(n, c):
        part = stiff.at[n, chaos, c]
        return remote(part, part, send_sem, recv_sem.at[n if n == 0 else n + c], partner)

    def exchange_some(n, c, j, count, sem):
        part = stiff.at[n, chaos, c, pl.ds(j, count)]
        return remote(part, part, send_sem, recv_sem.at[sem], partner)

    def exchange_tail(n):
        return exchange_some(last, comps - 1, *TAIL[n], last + comps - 1 + n)

    def exchange_block(n):
        part = stiff.at[n, chaos]
        return remote(part, part, send_sem, recv_sem.at[n], partner)

    lane = lax.broadcasted_iota(jnp.int32, (8, 128), 1)
    first_lane, last_lane = lane == 0, lane == 127

    def stencil(group, places, unroll, components=(0, 1, 2), span=(0, modes)):
        def body(j, carry):
            for c in components:
                for place in places:
                    z, at = place_of(group, place)
                    base = PAD + at * 8 * azims + z
                    face = pl.ds(at * 8, 8)

                    def layer(shift):
                        return u[j, c, pl.ds(base + shift, 8, stride=azims), :]

                    x = layer(0)
                    low = layer(-1) if z > 0 else azim_recv[1, j, c, face]
                    high = layer(1) if z < azims - 1 else azim_recv[0, j, c, face]
                    pairs = [
                        layer(azims) + layer(-azims),
                        low + high,
                        jnp.where(first_lane, 0.0, pltpu.roll(x, 1, 1))
                        + jnp.where(last_lane, 0.0, pltpu.roll(x, 127, 1)),
                    ]
                    total = pairs[(c + 1) % 3] + pairs[(c + 2) % 3] + 3.0 * pairs[c]
                    stiff[4 * group + place, chaos, c, j] = 10.0 * x - total
            return carry

        lax.fori_loop(*span, body, 0, unroll=unroll)

    def rows_of(group, place):
        z, at = place_of(group, place)
        return pl.ds(at * (8 * azims) + z, 8, stride=azims)

    def couple(cells, count, put):
        factors = [fields[k, cells, :] for k in range(terms)]

        def row(i, carry):
            mode = first_own + i
            total = [None] * count
            for k in range(terms):
                part = [None] * count
                for s in range(slots):
                    column, value = cols[k, s, mode], vals[k, s, mode]
                    for c in range(count):
                        term = value * work[c, column]
                        part[c] = term if s == 0 else part[c] + term
                for c in range(count):
                    scaled = factors[k] * part[c]
                    total[c] = scaled if k == 0 else total[c] + scaled
            for c in range(count):
                put(i, c, total[c])
            return carry

        lax.fori_loop(0, modes, row, 0)

    def finish(group, first, count):
        def block(place, carry):
            n = 4 * group + place
            cells = rows_of(group, place)

            exchange_block(n).wait_recv()

            def gather(j, carry):
                for half in range(2):
                    for c in range(comps):
                        work[c, half * modes + j] = stiff[n, half, c, j]
                return carry

            lax.fori_loop(0, modes, gather, 0, unroll=3)

            def put(i, c, value):
                out[i, c, cells, :] = value

            couple(cells, comps, put)
            return carry

        lax.fori_loop(first, first + count, block, 0)

    last_cells = rows_of(3, 3)
    zero = jnp.zeros((8, 128), F32)

    def begin_last():
        def gather(j, carry):
            for c in range(comps):
                work[c, first_own + j] = stiff[last, chaos, c, j]
                work[c, first_other + j] = zero
            return carry

        lax.fori_loop(0, modes, gather, 0, unroll=2)

        def put(i, c, value):
            out[i, c, last_cells, :] = value

        couple(last_cells, comps, put)

    def fill_matrix(first, count):
        def three(q, carry):
            def unit(j, carry):
                for c in range(comps):
                    work[c, j] = jnp.where(j == first_other + q * comps + c, zero + 1.0, zero)
                return carry

            lax.fori_loop(0, 2 * modes, unit, 0, unroll=4)

            def put(i, c, value):
                matrix[i, q * comps + c] = value

            couple(last_cells, comps, put)
            return carry

        lax.fori_loop(first, first + count, three, 0)

    def store(at, c):
        part = pl.ds(at * 8 * azims, 8 * azims)
        return pltpu.make_async_copy(out.at[:, c, part], out_any.at[:, c, part], store_sem)

    def finish_last():
        def take(c, first, count, unroll):
            values = [stiff[last, 1 - chaos, c, first + j] for j in range(count)]

            def row(i, carry):
                sums = [out[i, c, last_cells, :], zero, zero]
                for j in range(count):
                    sums[j % 3] = sums[j % 3] + matrix[i, first + j] * values[j]
                out[i, c, last_cells, :] = sums[0] + (sums[1] + sums[2])
                return carry

            lax.fori_loop(0, modes, row, 0, unroll=unroll)

        def piece(c, carry):
            exchange(last, c).wait_recv()
            take(c, 0, modes, 3)
            store(3, c).start()
            return carry

        lax.fori_loop(0, comps - 1, piece, 0)
        for n, (first, count) in enumerate(TAIL):
            exchange_tail(n).wait_recv()
            take(comps - 1, first, count, 18 // count)
        store(3, comps - 1).start()

    @pl.when(even)
    def _():
        pl.semaphore_wait(barrier, 3)

    @pl.when(jnp.logical_and(odd, jnp.logical_not(cut_before)))
    def _():
        pl.semaphore_wait(barrier, 5)

    @pl.when(cut_before)
    def _():
        pl.semaphore_wait(barrier, 4)

    @pl.when(has_prev)
    def _():
        axial_copies[0].start()

    @pl.when(has_next)
    def _():
        axial_copies[1].start()

    for copy in loads[4:] + later:
        copy.start()
    loads[0].wait()
    stencil(0, (0,), FEW, (0,), (0, FEW))
    exchange_some(0, 0, 0, FEW, 0).start()
    loads[1].wait()
    stencil(0, (0,), modes - FEW, (0,), (FEW, modes))
    exchange_some(0, 0, FEW, modes - FEW, 0).start()
    loads[2].wait()
    stencil(0, (0,), 9, (1, 2))
    exchange(0, 1).start()
    exchange(0, 2).start()

    @pl.when(odd)
    def _():
        pl.semaphore_signal(hello, inc=1, device_id=azim_prev, device_id_type=MESH)

    @pl.when(jnp.logical_and(odd, jnp.logical_not(cut_before)))
    def _():
        pl.semaphore_signal(hello, inc=1, device_id=azim_next, device_id_type=MESH)

    stencil(0, (1,), 6)
    exchange_block(1).start()
    rest = sum(load[-1] for load in LOADS[3:])
    pltpu.make_async_copy(
        u_hbm.at[:, :, pl.ds(0, rest)], u.at[:, :, pl.ds(PAD, rest)], load_sem.at[3]
    ).wait()
    stencil(0, (2, 3), 3)
    exchange_block(2).start()
    exchange_block(3).start()

    def pack_azim(j, carry):
        for c in range(comps):
            for at in range(axials // 8):
                for s, z in ((0, 0), (1, azims - 1)):
                    azim_send[s, j, c, pl.ds(at * 8, 8)] = u[
                        j, c, pl.ds(PAD + at * 8 * azims + z, 8, stride=azims), :]
        return carry

    lax.fori_loop(0, modes, pack_azim, 0)

    for has, s, first in ((has_prev, 1, PAD - azims), (has_next, 0, PAD + rows)):
        @pl.when(has)
        def _(s=s, first=first):
            axial_copies[s].wait_recv()

            def unpack(j, carry):
                for c in range(comps):
                    u[j, c, first:first + azims, :] = axial_recv[s, j, c]
                return carry

            lax.fori_loop(0, modes, unpack, 0, unroll=3)

        @pl.when(jnp.logical_not(has))
        def _(first=first):
            def clear(j, carry):
                for c in range(comps):
                    u[j, c, first:first + azims, :] = jnp.zeros((azims, 128), F32)
                return carry

            lax.fori_loop(0, modes, clear, 0, unroll=3)

    stencil(1, range(4), 2)
    for n in range(4, 8):
        exchange_block(n).start()

    @pl.when(even)
    def _():
        pl.semaphore_wait(hello, 2)

    @pl.when(relays)
    def _():
        for target in (partner, {**partner, **azim_prev}):
            pl.semaphore_signal(hello, inc=1, device_id=target, device_id_type=MESH)

    @pl.when(cut_before)
    def _():
        pl.semaphore_wait(hello, 1)

    for copy in azim_copies:
        copy.start()
    whole = fields.at[:, pl.ds(0, rows)]
    pltpu.make_async_copy(whole, whole, load_sem.at[4]).wait()
    for copy in later[2:]:
        copy.wait()
    finish(0, 0, 4)
    finish(1, 0, 1)
    for copy in azim_copies:
        copy.wait_recv()
    stencil(2, range(4), 2)
    for n in range(8, 12):
        exchange_block(n).start()
    stencil(3, range(4), 2)
    for n in range(12, last):
        exchange_block(n).start()
    for c in range(comps - 1):
        exchange(last, c).start()
    for n in range(len(TAIL)):
        exchange_tail(n).start()
    finish(1, 1, 3)
    begin_last()
    fill_matrix(0, 3)
    finish(2, 0, 4)
    for at in range(2):
        for c in range(comps):
            store(at, c).start()
    fill_matrix(3, 3)

    finish(3, 0, 2)
    for c in range(comps):
        store(2, c).start()
    finish(3, 2, 1)
    finish_last()

    @pl.when(has_prev)
    def _():
        axial_copies[0].wait_send()

    @pl.when(has_next)
    def _():
        axial_copies[1].wait_send()

    remote(azim_send, azim_recv, azim_ssem, azim_rsem.at[0], azim_next).wait_send()
    every = stiff.at[:, chaos]
    remote(every, every, send_sem, recv_sem.at[0], partner).wait_send()
    pltpu.make_async_copy(out.at[:, :, pl.ds(0, rows)], out_any, store_sem).wait()


def on_device(displacement, mean_modulus, kl_fields, triple_cols, triple_vals):
    modes, comps, axials, azims, radials = displacement.shape
    terms, all_modes, slots = triple_cols.shape
    rows = axials * azims
    dma = pltpu.SemaphoreType.DMA
    result = pl.pallas_call(
        functools.partial(kernel, (modes, comps, axials, azims, terms, slots)),
        out_shape=jax.ShapeDtypeStruct((modes, comps, rows, radials), F32),
        in_specs=[pl.BlockSpec(memory_space=pltpu.HBM)] * 6,
        out_specs=pl.BlockSpec(memory_space=pl.ANY),
        scratch_shapes=[
            pltpu.VMEM((modes, comps, rows + 2 * PAD, radials), F32),
            pltpu.VMEM((terms, rows + PAD, radials), F32),
            pltpu.SMEM((terms, slots, all_modes), jnp.int32),
            pltpu.SMEM((terms, slots, all_modes), F32),
            pltpu.VMEM((2, modes, comps, axials, radials), F32),
            pltpu.VMEM((2, modes, comps, axials, radials), F32),
            pltpu.VMEM((2, modes, comps, azims, radials), F32),
            pltpu.VMEM((16, 2, comps, modes, 8, radials), F32),
            pltpu.VMEM((comps, 2 * modes, 8, radials), F32),
            pltpu.VMEM((modes, modes, 8, radials), F32),
            pltpu.VMEM((modes, comps, rows + PAD, radials), F32),
            dma((7,)), dma(()), dma(()), dma((2,)), dma((2,)), dma((2,)),
            dma(()), dma((20,)), pltpu.SemaphoreType.REGULAR,
        ],
        compiler_params=pltpu.CompilerParams(
            collective_id=0, has_side_effects=True, vmem_limit_bytes=32 * 2**20
        ),
    )(*(
        pltpu.with_memory_space_constraint(x, pltpu.HBM)
        for x in (
            displacement.reshape(modes, comps, rows, radials),
            displacement,
            mean_modulus.reshape(1, rows, radials),
            kl_fields.reshape(terms - 1, rows, radials),
            triple_cols.transpose(0, 2, 1),
            triple_vals.transpose(0, 2, 1),
        )
    ))
    return result.reshape(displacement.shape)


def solution(mesh):
    return jax.shard_map(
        on_device,
        mesh=mesh,
        in_specs=(
            P("chaos", None, "axial", "azim", None),
            P("axial", "azim", None),
            P(None, "axial", "azim", None),
            P(),
            P(),
        ),
        out_specs=P("chaos", None, "axial", "azim", None),
        check_vma=False,
    )
```
